512 devices in a mesh: ctx: 64 (over x, y, core), kvh: 8 (over z).
Axes of the slice: x: 4, y: 8, z: 8, core: 2. Of those that a mesh axis runs over, the one named last changes fastest.
Arguments:
- ctx_q: bfloat16 [8192, 8192], P('ctx', 'kvh'), may hold values from -160 to 160
- ctx_kv: bfloat16 [2, 8192, 1024], P(None, 'ctx', 'kvh'), may hold values from -6 to 6
- quest_q: bfloat16 [64, 128, 8192], P('ctx', None, 'kvh'), may hold values from -160 to 160
- quest_kv: bfloat16 [64, 2, 128, 1024], P('ctx', None, None, 'kvh'), may hold values from -6 to 6
- quest_len: int32 [1], replicated, may hold values from 64 to 128
- host_block: int32 [1], replicated, may hold values from 1 to 63
- out_weight: bfloat16 [8192, 8192], P('kvh', 'ctx'), may hold values from -0.0625 to 0.0625
Outputs:
- ctx_out: bfloat16 [8192, 8192], P('ctx', 'kvh')
- quest_out: bfloat16 [128, 8192], P('kvh', 'ctx')
The draws below stay inside these ranges and needn't reach their ends.
All inputs are finite; a program needn't handle non-finite values.
Results may differ from the reference program's by a relative error of at most 0.019.
Values may be sent and summed in bfloat16 or wider, within the bound.
A program may use at most 192 MiB of HBM per device.

```python
import jax
import jax.numpy as jnp
from jax import lax

HQ = 64
KVH = 8
DH = 128
D = 8192
BLK = 128
QMAX = 128
CTX_TOKENS = 8192
N_CTX = 64


def base_keys(key):
    values = jax.random.normal(jax.random.fold_in(key, 900), (CTX_TOKENS, KVH * DH), jnp.float32)
    return jnp.clip(values, -6.0, 6.0)


def draw_ctx_kv(key, part):
    key_rows = base_keys(key)
    key = jax.random.fold_in(key, 1)
    val_rows = jnp.clip(jax.random.normal(key, (CTX_TOKENS, KVH * DH), jnp.float32), -6.0, 6.0)
    return jnp.stack([key_rows, val_rows]).astype(jnp.bfloat16)


def draw_ctx_q(key, part):
    key = jax.random.fold_in(key, 2)
    queries = jnp.clip(jax.random.normal(key, (CTX_TOKENS, HQ * DH), jnp.float32), -6.0, 6.0)
    return queries.astype(jnp.bfloat16)


def draw_quest_q(key, part):
    key = jax.random.fold_in(key, 3)
    queries = jnp.clip(jax.random.normal(key, (N_CTX, QMAX, HQ * DH), jnp.float32), -6.0, 6.0)
    return queries.astype(jnp.bfloat16)


def shard_levels(stream_key, extent, cuts, smallest, largest):
    level = 1.0
    for dim, shards_of in cuts:
        steps = jax.random.uniform(jax.random.fold_in(jax.random.fold_in(stream_key, 6), dim), (shards_of,), jnp.float32, smallest / len(cuts), largest / len(cuts))
        level = level * jnp.repeat(jnp.exp(steps), extent[dim] // shards_of).reshape((-1,) + (1,) * (len(extent) - 1 - dim))
    return level


def bell_draw(stream_key, dims, scale, limit, cuts=(), held_as=jnp.bfloat16):
    level = shard_levels(stream_key, dims, cuts, -0.22, 0.18) if cuts else 1.0
    result = jax.random.normal(stream_key, dims, jnp.float32) * scale * level
    return jnp.minimum(jnp.maximum(result, -limit), limit).astype(held_as)


def setup_inputs(seed: int = 0) -> dict:
    streams_of = jax.random.split(jax.random.key(seed), 8)
    return {
        "ctx_q": draw_ctx_q(jax.random.fold_in(streams_of[7], 71), 0),
        "ctx_kv": draw_ctx_kv(jax.random.fold_in(streams_of[7], 71), 0),
        "quest_q": draw_quest_q(jax.random.fold_in(streams_of[7], 71), 0),
        "quest_kv": bell_draw(streams_of[3], (N_CTX, 2, QMAX, KVH * DH), 1.0, 6.0, ((0, 64), (3, 8))),
        "quest_len": jax.random.randint(streams_of[4], (1,), QMAX // 2, QMAX + 1).astype(jnp.int32),
        "host_block": jax.random.randint(streams_of[5], (1,), 1, N_CTX).astype(jnp.int32),
        "out_weight": bell_draw(streams_of[6], (HQ * DH, D), (HQ * DH) ** -0.5, 0.0625, ((0, 8), (1, 64))),
    }


MASKED = -1.0e30


def head_scores(queries, key_rows, visible):
    scores = jnp.dot(queries, key_rows.T, preferred_element_type=jnp.float32) * (DH ** -0.5)
    return jnp.where(visible, scores, MASKED)


def attend_heads(queries, key_rows, val_rows, visible, group):
    heads = queries.shape[1] // DH
    output = jnp.zeros(queries.shape, jnp.bfloat16)

    def loop_body(head_idx, output):
        query_head = lax.dynamic_slice_in_dim(queries, head_idx * DH, DH, 1)
        key_head = lax.dynamic_slice_in_dim(key_rows, (head_idx // group) * DH, DH, 1)
        val_head = lax.dynamic_slice_in_dim(val_rows, (head_idx // group) * DH, DH, 1)
        scores = head_scores(query_head, key_head, visible)
        maximum = jnp.max(scores, axis=1, keepdims=True)
        weights = jnp.exp(scores - maximum)
        totals = jnp.sum(weights, axis=1, keepdims=True)
        numer = jnp.dot(weights.astype(jnp.bfloat16), val_head, preferred_element_type=jnp.float32)
        return lax.dynamic_update_slice_in_dim(output, (numer / totals).astype(jnp.bfloat16), head_idx * DH, 1)

    return lax.fori_loop(0, heads, loop_body, output)


def partial_heads(queries, key_rows, val_rows, visible, group):
    heads = queries.shape[1] // DH
    rows_n = queries.shape[0]
    start_state = (jnp.zeros((rows_n, heads), jnp.float32), jnp.zeros((rows_n, heads), jnp.float32),
                   jnp.zeros((rows_n, heads * DH), jnp.float32))

    def loop_body(head_idx, state):
        maxima, totals, numers = state
        query_head = lax.dynamic_slice_in_dim(queries, head_idx * DH, DH, 1)
        key_head = lax.dynamic_slice_in_dim(key_rows, (head_idx // group) * DH, DH, 1)
        val_head = lax.dynamic_slice_in_dim(val_rows, (head_idx // group) * DH, DH, 1)
        scores = head_scores(query_head, key_head, visible)
        maximum = jnp.max(scores, axis=1)
        weights = jnp.exp(scores - maximum[:, None])
        total = jnp.sum(weights, axis=1)
        numer = jnp.dot(weights.astype(jnp.bfloat16), val_head, preferred_element_type=jnp.float32)
        maxima = lax.dynamic_update_slice_in_dim(maxima, maximum[:, None], head_idx, 1)
        totals = lax.dynamic_update_slice_in_dim(totals, total[:, None], head_idx, 1)
        numers = lax.dynamic_update_slice_in_dim(numers, numer, head_idx * DH, 1)
        return (maxima, totals, numers)

    return lax.fori_loop(0, heads, loop_body, start_state)


def combine_states(first, second):
    max_a, tot_a, num_a = first
    max_b, tot_b, num_b = second
    joined = jnp.maximum(max_a, max_b)
    fac_a = jnp.exp(max_a - joined)
    fac_b = jnp.exp(max_b - joined)
    width = num_a.shape[1] // max_a.shape[1]
    numers = num_a * jnp.repeat(fac_a, width, axis=1) + num_b * jnp.repeat(fac_b, width, axis=1)
    return (joined, tot_a * fac_a + tot_b * fac_b, numers)


def reference(ctx_q, ctx_kv, quest_q, quest_kv, quest_len, host_block, out_weight):
    group = HQ // KVH
    anchor_keys = ctx_kv[0, :BLK]
    anchor_vals = ctx_kv[1, :BLK]
    row_ids = jnp.arange(BLK, dtype=jnp.int32)[:, None]
    col_ids = jnp.arange(2 * BLK, dtype=jnp.int32)[None, :]

    def one_block(block):
        first = (block * BLK).astype(jnp.int32)
        queries = lax.dynamic_slice_in_dim(ctx_q, first, BLK, 0)
        key_rows = jnp.concatenate([anchor_keys, lax.dynamic_slice_in_dim(ctx_kv[0], first, BLK, 0)], axis=0)
        val_rows = jnp.concatenate([anchor_vals, lax.dynamic_slice_in_dim(ctx_kv[1], first, BLK, 0)], axis=0)
        visible = jnp.where(col_ids < BLK, block > 0, col_ids - BLK <= row_ids)
        return attend_heads(queries, key_rows, val_rows, visible, group)

    ctx_out = lax.map(one_block, jnp.arange(N_CTX, dtype=jnp.int32)).reshape(CTX_TOKENS, HQ * DH)

    host = host_block[0]
    question = lax.dynamic_index_in_dim(quest_q, host, 0, keepdims=False)
    own_kv = lax.dynamic_index_in_dim(quest_kv, host, 0, keepdims=False)
    all_visible = jnp.ones((QMAX, BLK), dtype=bool)
    start_state = (jnp.full((QMAX, HQ), MASKED, jnp.float32), jnp.zeros((QMAX, HQ), jnp.float32),
                   jnp.zeros((QMAX, HQ * DH), jnp.float32))

    def scan_block(state, block):
        first = (block * BLK).astype(jnp.int32)
        key_rows = lax.dynamic_slice_in_dim(ctx_kv[0], first, BLK, 0)
        val_rows = lax.dynamic_slice_in_dim(ctx_kv[1], first, BLK, 0)
        part = partial_heads(question, key_rows, val_rows, all_visible, group)
        return combine_states(state, part), None

    state, unused = lax.scan(scan_block, start_state, jnp.arange(N_CTX, dtype=jnp.int32))
    q_rows = jnp.arange(QMAX, dtype=jnp.int32)[:, None]
    q_cols = jnp.arange(QMAX, dtype=jnp.int32)[None, :]
    own_visible = (q_cols <= q_rows) & (q_cols < quest_len[0])
    state = combine_states(state, partial_heads(question, own_kv[0], own_kv[1], own_visible, group))
    maxima, totals, numers = state
    attn = numers / jnp.repeat(totals, DH, axis=1)
    attn = jnp.where(q_rows < quest_len[0], attn, 0.0).astype(jnp.bfloat16)
    quest_out = jnp.dot(attn, out_weight, preferred_element_type=jnp.float32).astype(jnp.bfloat16)
    return ctx_out, quest_out
```

```python
import math

import jax
import jax.numpy as jnp
from jax import lax
from jax.experimental import pallas as pl
from jax.experimental.pallas import tpu as pltpu
from jax.sharding import PartitionSpec as P


DH = 128
BLK = 128
HEADS = 8
HALF = 64
NX, NY, NZ = 4, 8, 8
GROUP = 16
NPG = 4
MASKED = -1e30
SCALE = DH ** (-0.5)
LOG2E = math.log2(math.e)
COEF = SCALE * LOG2E
MESH = pl.DeviceIdType.MESH


def dot_t(a, b):
    return lax.dot_general(a, b, (((1,), (1,)), ((), ())), preferred_element_type=jnp.float32)


def kernel(
    len_ref, host_ref, cq_hbm, ckv_hbm, qq_hbm, qkv_hbm, w_hbm,
    cout_hbm, qout_ref,
    cq, w, akv, kvall, q1buf, q1sel, q2buf, r1buf, r1sel, pbuf, lbuf, abuf, zsrc, zbuf, cout,
    lsem, osem, q1_s, q1_r, q2_s, q2_r, r1_s, r1_r, r2_s, r2_r, kv_s, kv_r, km_s, km_r,
    a1_s, a1_r, a2_s, a2_r, am_s, am_r, p_s, p_r, l_s, l_r, g_s, g_r, z_s, z_r,
):
    ctx = lax.axis_index("ctx")
    z = lax.axis_index("kvh")
    x = ctx // 16
    y = (ctx // 2) % NY
    c = ctx % 2
    yp = y % 2
    pg = y // 2
    head = x * 2 + c
    gid = c * 8 + x * 2 + yp

    def at(x2, y2, c2, z2):
        return ((x2 * NY + y2) * 2 + c2, z2)

    group = []
    for dx in range(NX):
        for dp in range(2):
            for dc in range(2):
                if dx or dp or dc:
                    x2 = (x + dx) % NX
                    yp2 = (yp + dp) % 2
                    c2 = (c + dc) % 2
                    group.append((dx, dp, dc, x2, yp2, c2, at(x2, pg * 2 + yp2, c2, z)))
    across = [at(x, (y + 2 * k) % NY, c, z) for k in range(1, NPG)]
    heads_z = [((z + k) % NZ, at(x, y, c, (z + k) % NZ)) for k in range(1, NZ)]
    mate = at(x, y, 1 - c, z)

    def local(src, dst, sem):
        cp = pltpu.make_async_copy(src, dst, sem)
        cp.start()
        return cp

    def send(src, dst, ssem, rsem, target):
        pltpu.make_async_remote_copy(
            src_ref=src, dst_ref=dst, send_sem=ssem, recv_sem=rsem, device_id=target, device_id_type=MESH
        ).start()

    def drain(ref, sem):
        pltpu.make_async_copy(ref, ref, sem).wait()

    load_q = local(cq_hbm, cq, lsem.at[0])
    load_own = local(ckv_hbm, akv.at[:, pl.ds(BLK, BLK), :], lsem.at[1])
    load_w = local(w_hbm, w, lsem.at[2])

    barrier = pltpu.get_barrier_semaphore()
    for member in group:
        pl.semaphore_signal(barrier, inc=1, device_id=member[-1], device_id_type=MESH)
    for target in across:
        pl.semaphore_signal(barrier, inc=1, device_id=target, device_id_type=MESH)
    for _, target in heads_z:
        pl.semaphore_signal(barrier, inc=1, device_id=target, device_id_type=MESH)
    pl.semaphore_wait(barrier, len(group) + len(across) + len(heads_z))

    def q_piece(x2, yp2, c2):
        return qq_hbm.at[0, pl.ds(pl.multiple_of(HALF * yp2, HALF), HALF),
                         pl.ds(pl.multiple_of(DH * (x2 * 2 + c2), DH), DH)]

    def kv_piece(x2, yp2, c2):
        return qkv_hbm.at[0, c2, pl.ds(pl.multiple_of(16 * (x2 * 2 + yp2), 16), 16), :]

    def block_rows(g):
        return kvall.at[:, pl.ds(pl.multiple_of(BLK * g, BLK), BLK), :]

    for dx, dp, dc, x2, yp2, c2, target in group:
        send(q_piece(x2, yp2, c2), q1buf.at[gid], q1_s, q1_r, target)
    local(q_piece(x, yp, c), q1buf.at[gid], q1_r)
    for dx, dp, dc, x2, yp2, c2, target in group:
        send(kv_piece(x2, yp2, c2), r1buf.at[gid], r1_s, r1_r, target)
    local(kv_piece(x, yp, c), r1buf.at[gid], r1_r)

    @pl.when(ctx == 0)
    def _():
        for target in across:
            send(ckv_hbm, akv.at[:, pl.ds(0, BLK), :], a1_s, a1_r, target)
        local(ckv_hbm, akv.at[:, pl.ds(0, BLK), :], a1_r)

    for dx, dp, dc, x2, yp2, c2, target in group:
        if dc == 0:
            send(ckv_hbm, block_rows(gid), kv_s, kv_r, target)
    local(ckv_hbm, block_rows(gid), kv_r)

    host = host_ref[0]
    length = len_ref[0]
    host_y = (host // 2) % NY
    host_pg = host_y // 2
    host_g = (host % 2) * 8 + (host // 16) * 2 + host_y % 2

    drain(q1buf, q1_r)
    q1sel[...] = q1buf[host_g]
    for target in across:
        send(q1sel, q2buf.at[pg], q2_s, q2_r, target)
    local(q1sel, q2buf.at[pg], q2_r)

    drain(r1buf, r1_r)
    r1sel[...] = r1buf[host_g]
    r2dst = kvall.at[c, pl.ds(pl.multiple_of(GROUP * BLK + 16 * (x * 2 + yp), 16), 16), :]
    for dx, dp, dc, x2, yp2, c2, target in group:
        send(r1sel, r2dst, r2_s, r2_r, target)
    local(r1sel, r2dst, r2_r)

    half_blocks = kvall.at[:, pl.ds(pl.multiple_of(8 * BLK * c, BLK), 8 * BLK), :]
    drain(half_blocks, kv_r)
    send(half_blocks, half_blocks, km_s, km_r, mate)

    is_source = (x == 0) & (yp == 0) & (c == 0)
    anchor_rows = akv.at[:, pl.ds(0, BLK), :]

    @pl.when(is_source)
    def _():
        drain(anchor_rows, a1_r)
        for dx, dp, dc, x2, yp2, c2, target in group:
            if dc == 0:
                send(anchor_rows, anchor_rows, a2_s, a2_r, target)

    drain(q2buf, q2_r)
    drain(kvall.at[:, pl.ds(GROUP * BLK, BLK), :], r2_r)
    drain(half_blocks, km_r)

    qsel = q2buf[host_pg]
    raw = dot_t(qsel, kvall[0])
    keys_n = (GROUP + 1) * BLK
    col = lax.broadcasted_iota(jnp.int32, (HALF, BLK), 1)
    row = lax.broadcasted_iota(jnp.int32, (HALF, BLK), 0) + HALF * yp
    limit = jnp.where(host_pg == pg, length, 0)
    own = jnp.where((col <= row) & (col < limit), raw[:, GROUP * BLK:], MASKED)
    raw = jnp.concatenate([raw[:, : GROUP * BLK], own], axis=1)
    top = jnp.max(raw, axis=1, keepdims=True)
    wts = jnp.exp2((raw - top) * COEF)
    tot = jnp.sum(wts, axis=1, keepdims=True)
    num = jnp.dot(wts.astype(jnp.bfloat16), kvall[1], preferred_element_type=jnp.float32)
    pbuf[pg] = (num / tot).astype(jnp.bfloat16)
    lse = top * COEF + jnp.log(tot) * LOG2E
    row64 = lax.broadcasted_iota(jnp.int32, (HALF, BLK), 0)
    diag = col == row64
    lse_row = jnp.sum(jnp.where(diag, lse, 0.0), axis=0, keepdims=True)
    lbuf[pg] = jnp.broadcast_to(lse_row, (8, BLK))
    for target in across:
        send(lbuf.at[pg], lbuf.at[pg], l_s, l_r, target)
        send(pbuf.at[pg], pbuf.at[pg], p_s, p_r, target)

    @pl.when(c == 0)
    def _():
        @pl.when(jnp.logical_not(is_source))
        def _():
            drain(anchor_rows, a2_r)

        send(anchor_rows, anchor_rows, am_s, am_r, mate)

    load_q.wait()
    load_own.wait()

    drain(lbuf.at[pl.ds(0, 3)], l_r)
    drain(pbuf.at[pl.ds(0, 3)], p_r)
    rows4 = [lbuf[i][0:1, :] for i in range(NPG)]
    best = jnp.maximum(jnp.maximum(rows4[0], rows4[1]), jnp.maximum(rows4[2], rows4[3]))
    fac = [jnp.exp2(r - best) for r in rows4]
    inv = 1.0 / (fac[0] + fac[1] + fac[2] + fac[3])
    attn = jnp.zeros((HALF, DH), jnp.float32)
    for i in range(NPG):
        fcol = jnp.sum(jnp.where(diag, fac[i] * inv, 0.0), axis=1, keepdims=True)
        attn = attn + fcol * pbuf[i].astype(jnp.float32)
    attn = jnp.where(row < length, attn, 0.0).astype(jnp.bfloat16)
    mine = abuf.at[pl.ds(pl.multiple_of(HALF * yp, HALF), HALF), pl.ds(pl.multiple_of(DH * head, DH), DH)]
    mine[...] = attn
    for dx, dp, dc, x2, yp2, c2, target in group:
        send(mine, mine, g_s, g_r, target)

    @pl.when(c == 1)
    def _():
        drain(anchor_rows, am_r)

    ccol = lax.broadcasted_iota(jnp.int32, (BLK, 2 * BLK), 1)
    crow = lax.broadcasted_iota(jnp.int32, (BLK, 2 * BLK), 0)
    first_visible = jnp.where(ctx > 0, 0, BLK)
    visible = (ccol >= first_visible) & (ccol - BLK <= crow)

    def context_heads(lo, hi):
        for h in range(lo, hi):
            sc = dot_t(cq[:, h * DH:(h + 1) * DH], akv[0])
            sc = jnp.where(visible, sc, MASKED)
            mx = jnp.max(sc, axis=1, keepdims=True)
            pw = jnp.exp2((sc - mx) * COEF)
            tl = jnp.sum(pw, axis=1, keepdims=True)
            nm = jnp.dot(pw.astype(jnp.bfloat16), akv[1], preferred_element_type=jnp.float32)
            cout[:, h * DH:(h + 1) * DH] = (nm / tl).astype(jnp.bfloat16)

    context_heads(0, 4)

    load_w.wait()
    drain(q1buf.at[pl.ds(0, GROUP - 1)], g_r)
    zsrc[...] = jnp.dot(abuf[...], w[...], preferred_element_type=jnp.float32).astype(jnp.bfloat16)
    for z2, target in heads_z:
        send(zsrc.at[pl.ds(pl.multiple_of(16 * z2, 16), 16), :], zbuf.at[z], z_s, z_r, target)
    zbuf[z] = zsrc[pl.ds(pl.multiple_of(16 * z, 16), 16), :]

    context_heads(4, 8)
    store_c = local(cout, cout_hbm, osem)

    drain(q1buf.at[pl.ds(0, GROUP - 1)], q1_s)
    drain(r1buf.at[pl.ds(0, GROUP - 1)], r1_s)
    drain(r1buf.at[pl.ds(0, GROUP - 1)], r2_s)
    drain(kvall.at[:, pl.ds(0, 7 * BLK), :], kv_s)
    drain(half_blocks, km_s)
    drain(q2buf.at[pl.ds(0, 3)], q2_s)
    drain(pbuf.at[pl.ds(0, 3)], p_s)
    drain(lbuf.at[pl.ds(0, 3)], l_s)
    drain(q1buf.at[pl.ds(0, GROUP - 1)], g_s)

    @pl.when(ctx == 0)
    def _():
        drain(kvall.at[:, pl.ds(0, 3 * BLK), :], a1_s)

    @pl.when(is_source)
    def _():
        drain(kvall.at[:, pl.ds(0, 7 * BLK), :], a2_s)

    @pl.when(c == 0)
    def _():
        drain(anchor_rows, am_s)

    drain(zbuf.at[pl.ds(0, 7)], z_r)
    total = zbuf[0].astype(jnp.float32)
    for i in range(1, NZ):
        total = total + zbuf[i].astype(jnp.float32)
    qout_ref[...] = total.astype(jnp.bfloat16)
    drain(zbuf.at[pl.ds(0, 7)], z_s)
    store_c.wait()


def per_device(ctx_q, ctx_kv, quest_q, quest_kv, quest_len, host_block, out_weight):
    bf = jnp.bfloat16
    any_spec = pl.BlockSpec(memory_space=pl.ANY)
    smem = pl.BlockSpec(memory_space=pltpu.SMEM)
    dma = pltpu.SemaphoreType.DMA
    return pl.pallas_call(
        kernel,
        out_shape=(
            jax.ShapeDtypeStruct((BLK, HEADS * DH), bf),
            jax.ShapeDtypeStruct((BLK // NZ, DH), bf),
        ),
        in_specs=[smem, smem] + [any_spec] * 5,
        out_specs=(any_spec, pl.BlockSpec(memory_space=pltpu.VMEM)),
        scratch_shapes=[
            pltpu.VMEM((BLK, HEADS * DH), bf),
            pltpu.VMEM((HEADS * DH, DH), bf),
            pltpu.VMEM((2, 2 * BLK, DH), bf),
            pltpu.VMEM((2, (GROUP + 1) * BLK, DH), bf),
            pltpu.VMEM((GROUP, HALF, DH), bf),
            pltpu.VMEM((HALF, DH), bf),
            pltpu.VMEM((NPG, HALF, DH), bf),
            pltpu.VMEM((GROUP, 16, DH), bf),
            pltpu.VMEM((16, DH), bf),
            pltpu.VMEM((NPG, HALF, DH), bf),
            pltpu.VMEM((NPG, 8, DH), jnp.float32),
            pltpu.VMEM((BLK, HEADS * DH), bf),
            pltpu.VMEM((BLK, DH), bf),
            pltpu.VMEM((NZ, 16, DH), bf),
            pltpu.VMEM((BLK, HEADS * DH), bf),
            dma((3,)),
        ] + [dma] * 27,
        compiler_params=pltpu.CompilerParams(
            collective_id=0, has_side_effects=True, vmem_limit_bytes=48 * 1024 * 1024
        ),
        name="star_attention",
    )(quest_len, host_block, ctx_q, ctx_kv, quest_q, quest_kv, out_weight)


def solution(mesh):
    return jax.shard_map(
        per_device,
        mesh=mesh,
        in_specs=(
            P("ctx", "kvh"),
            P(None, "ctx", "kvh"),
            P("ctx", None, "kvh"),
            P("ctx", None, None, "kvh"),
            P(),
            P(),
            P("kvh", "ctx"),
        ),
        out_specs=(P("ctx", "kvh"), P("kvh", "ctx")),
        check_vma=False,
    )
```

```python
import functools
import math

import jax
import jax.numpy as jnp
from jax import lax
from jax.experimental import pallas as pl
from jax.experimental.pallas import tpu as pltpu
from jax.sharding import PartitionSpec as P


DH = 128
BLK = 128
HEADS = 8
HALF = 64
NX, NY, NZ = 4, 8, 8
ROW = 8
NPG = 4
MASKED = -1e30
SCALE = DH ** (-0.5)
LOG2E = math.log2(math.e)
COEF = SCALE * LOG2E
MESH = pl.DeviceIdType.MESH


def dot_t(a, b):
    return lax.dot_general(a, b, (((1,), (1,)), ((), ())), preferred_element_type=jnp.float32)


def when(cond):
    if cond is None:
        return lambda f: f()
    return pl.when(cond)


def kernel(
    hx, hpg,
    len_ref, host_ref, cq_hbm, ckv_hbm, qq_hbm, qkv_hbm, w_hbm,
    cout_hbm, qout_ref,
    cq, w, akv, kvall, q1buf, q1sel, q2buf, r1buf, r1sel, po, lsend, pbuf, lbuf, abuf, zsrc, zbuf, cout,
    lsem, zs, osem, q1_s, q1_r, q2_s, q2_r, r1_s, r1_r, r2_s, r2_r, kv_s, kv_r, km_s, km_r,
    a1_s, a1_r, a2_s, a2_r, am_s, am_r, p_s, p_r, l_s, l_r, g_s, g_r, z_s, z_r,
):
    ctx = lax.axis_index("ctx")
    z = lax.axis_index("kvh")
    x = ctx // 16
    y = (ctx // 2) % NY
    c = ctx % 2
    yp = y % 2
    pg = y // 2
    head = x * 2 + c

    def at(x2, y2, c2, z2):
        return ((x2 * NY + y2) * 2 + c2, z2)

    group = []
    for dx in (1, 3, 2, 0):
        for dp in range(2):
            for dc in range(2):
                if dx or dp or dc:
                    x2 = (x + dx) % NX
                    yp2 = (yp + dp) % 2
                    c2 = (c + dc) % 2
                    group.append((dp, dc, x2, yp2, c2, at(x2, pg * 2 + yp2, c2, z)))
    row_members = [m[1:] for m in group if m[0] == 0]
    same_core = [m[-1] for m in row_members if m[0] == 0]
    column = [((yp + k) % 2, at(x, (y + k) % NY, c, z)) for k in (4, 3, 5, 2, 6, 1, 7)]
    heads_z = [((z + k) % NZ, at(x, y, c, (z + k) % NZ)) for k in (1, 7, 2, 6, 3, 5, 4)]
    z_near = [t for _, t in heads_z[:2]]
    mate = at(x, y, 1 - c, z)

    in_pg = None if hpg is None else pg == hpg
    sender = in_pg
    if hx is not None:
        sender = x == hx if sender is None else sender & (x == hx)
    q1_slots = 16 if hx is None else 4
    r1_slots = 8 if hx is None else 2
    q1_slot = c * 8 + x * 2 + yp if hx is None else c * 2 + yp
    r1_slot = c * 4 + x if hx is None else c

    def local(src, dst, sem):
        cp = pltpu.make_async_copy(src, dst, sem)
        cp.start()
        return cp

    def send(src, dst, ssem, rsem, target):
        pltpu.make_async_remote_copy(
            src_ref=src, dst_ref=dst, send_sem=ssem, recv_sem=rsem, device_id=target, device_id_type=MESH
        ).start()

    def drain(ref, sem):
        pltpu.make_async_copy(ref, ref, sem).wait()

    def halves(n):
        return kvall.at[0, pl.ds(0, n * HALF), :]

    def near_signal(i):
        for t in z_near:
            pl.semaphore_signal(zs.at[i], inc=1, device_id=t, device_id_type=MESH)

    load_q = local(cq_hbm, cq, lsem.at[0])
    load_own = local(ckv_hbm, akv.at[:, pl.ds(BLK, BLK), :], lsem.at[1])
    load_w = local(w_hbm, w, lsem.at[2])

    barrier = pltpu.get_barrier_semaphore()
    greet = [m[-1] for m in group] + [t for _, t in column] + z_near
    for t in greet:
        pl.semaphore_signal(barrier, inc=1, device_id=t, device_id_type=MESH)
    pl.semaphore_wait(barrier, len(greet))
    near_signal(0)

    def q_piece(x2, yp2, c2):
        return qq_hbm.at[0, pl.ds(pl.multiple_of(HALF * yp2, HALF), HALF),
                         pl.ds(pl.multiple_of(DH * (x2 * 2 + c2), DH), DH)]

    def kv_piece(x2, c2):
        first = pl.multiple_of(32 * (c2 * 2 + x2 % 2), 32)
        return qkv_hbm.at[0, x2 // 2, pl.ds(first, 32), :]

    block_rows = kvall.at[:, pl.ds(pl.multiple_of(BLK * (c * 4 + x), BLK), BLK), :]

    @when(sender)
    def _():
        for dc, x2, yp2, c2, target in row_members:
            send(kv_piece(x2, c2), r1buf.at[r1_slot], r1_s, r1_r, target)
        local(kv_piece(x, c), r1buf.at[r1_slot], r1_r)
        for dp, dc, x2, yp2, c2, target in group:
            send(q_piece(x2, yp2, c2), q1buf.at[q1_slot], q1_s, q1_r, target)
        local(q_piece(x, yp, c), q1buf.at[q1_slot], q1_r)

    for target in same_core:
        send(ckv_hbm, block_rows, kv_s, kv_r, target)
    local(ckv_hbm, block_rows, kv_r)

    anchor_rows = akv.at[:, pl.ds(0, BLK), :]

    @pl.when(ctx == 0)
    def _():
        for _, target in column:
            send(ckv_hbm, anchor_rows, a1_s, a1_r, target)
        local(ckv_hbm, anchor_rows, a1_r)

    host = host_ref[0]
    length = len_ref[0]
    host_x = host // 16
    host_y = (host // 2) % NY
    host_c = host % 2
    host_yp = host_y % 2
    host_q1 = host_c * 8 + host_x * 2 + host_yp if hx is None else host_c * 2 + host_yp
    host_r1 = host_c * 4 + host_x if hx is None else host_c

    own_rows = kvall.at[:, pl.ds(ROW * BLK, BLK), :]
    r2dst = kvall.at[x // 2, pl.ds(pl.multiple_of(ROW * BLK + 32 * (c * 2 + x % 2), 32), 32), :]
    half_blocks = kvall.at[:, pl.ds(pl.multiple_of(4 * BLK * c, BLK), 4 * BLK), :]
    q2dst = q2buf.at[pg if hpg is None else 0, pl.ds(pl.multiple_of(HALF * yp, HALF), HALF), :]

    @when(in_pg)
    def _():
        drain(r1buf, r1_r)
        r1sel[...] = r1buf[host_r1]
        for dc, x2, yp2, c2, target in row_members:
            send(r1sel, r2dst, r2_s, r2_r, target)
        local(r1sel, r2dst, r2_r)
        drain(q1buf, q1_r)
        q1sel[...] = q1buf[host_q1]
        for _, target in column:
            send(q1sel, q2dst, q2_s, q2_r, target)
        local(q1sel, q2dst, q2_r)

    if hpg is not None:
        @pl.when(pg != hpg)
        def _():
            own_rows[...] = jnp.zeros((2, BLK, DH), jnp.bfloat16)

    drain(half_blocks, kv_r)
    send(half_blocks, half_blocks, km_s, km_r, mate)

    is_source = (x == 0) & (c == 0)

    @pl.when(is_source)
    def _():
        drain(anchor_rows, a1_r)
        for target in same_core:
            send(anchor_rows, anchor_rows, a2_s, a2_r, target)

    pl.semaphore_wait(zs.at[0], 2)
    near_signal(1)

    drain(half_blocks, km_r)

    @when(in_pg)
    def _():
        drain(own_rows, r2_r)

    drain(q2buf, q2_r)

    qsel = q2buf[host_y // 2] if hpg is None else q2buf[0]
    raw = dot_t(qsel, kvall[0])
    col = lax.broadcasted_iota(jnp.int32, (BLK, BLK), 1)
    row = lax.broadcasted_iota(jnp.int32, (BLK, BLK), 0)
    limit = jnp.where(host_y == y, length, 0)
    own = jnp.where((col <= row) & (col < limit), raw[:, ROW * BLK:], MASKED)
    raw = jnp.concatenate([raw[:, : ROW * BLK], own], axis=1)
    top = jnp.max(raw, axis=1, keepdims=True)
    wts = jnp.exp2((raw - top) * COEF)
    tot = jnp.sum(wts, axis=1, keepdims=True)
    num = jnp.dot(wts.astype(jnp.bfloat16), kvall[1], preferred_element_type=jnp.float32)
    po[...] = (num / tot).astype(jnp.bfloat16)
    lse = top * COEF + jnp.log(tot) * LOG2E
    lse_row = jnp.sum(jnp.where(col == row, lse, 0.0), axis=0, keepdims=True)
    lse_tile = jnp.broadcast_to(lse_row, (8, BLK))
    lsend[...] = lse_tile
    lbuf[y] = lse_tile
    for h2, target in column:
        send(lsend, lbuf.at[y], l_s, l_r, target)
        send(po.at[pl.ds(pl.multiple_of(HALF * h2, HALF), HALF), :], pbuf.at[y], p_s, p_r, target)
    pbuf[y] = po[pl.ds(pl.multiple_of(HALF * yp, HALF), HALF), :]

    @pl.when(c == 0)
    def _():
        @pl.when(jnp.logical_not(is_source))
        def _():
            drain(anchor_rows, a2_r)

        send(anchor_rows, anchor_rows, am_s, am_r, mate)

    load_q.wait()
    load_own.wait()
    pl.semaphore_wait(zs.at[1], 2)
    near_signal(2)

    drain(lbuf.at[pl.ds(0, NY - 1)], l_r)
    drain(pbuf.at[pl.ds(0, NY - 1)], p_r)
    lses = [lbuf[i][0:1, :] for i in range(NY)]
    best = functools.reduce(jnp.maximum, lses)
    fac = [jnp.exp2(v - best) for v in lses]
    inv = 1.0 / functools.reduce(jnp.add, fac)
    hcol = lax.broadcasted_iota(jnp.int32, (HALF, BLK), 1)
    hrow = lax.broadcasted_iota(jnp.int32, (HALF, BLK), 0) + HALF * yp
    diag = hcol == hrow
    attn = jnp.zeros((HALF, DH), jnp.float32)
    for i in range(NY):
        fcol = jnp.sum(jnp.where(diag, fac[i] * inv, 0.0), axis=1, keepdims=True)
        attn = attn + fcol * pbuf[i].astype(jnp.float32)
    attn = jnp.where(hrow < length, attn, 0.0).astype(jnp.bfloat16)
    mine = abuf.at[pl.ds(pl.multiple_of(HALF * yp, HALF), HALF), pl.ds(pl.multiple_of(DH * head, DH), DH)]
    mine[...] = attn
    for dp, dc, x2, yp2, c2, target in group:
        send(mine, mine, g_s, g_r, target)

    @pl.when(c == 1)
    def _():
        drain(anchor_rows, am_r)

    ccol = lax.broadcasted_iota(jnp.int32, (BLK, 2 * BLK), 1)
    crow = lax.broadcasted_iota(jnp.int32, (BLK, 2 * BLK), 0)
    first_visible = jnp.where(ctx > 0, 0, BLK)
    visible = (ccol >= first_visible) & (ccol - BLK <= crow)

    def context_heads(lo, hi):
        for h in range(lo, hi):
            sc = dot_t(cq[:, h * DH:(h + 1) * DH], akv[0])
            sc = jnp.where(visible, sc, MASKED)
            mx = jnp.max(sc, axis=1, keepdims=True)
            pw = jnp.exp2((sc - mx) * COEF)
            tl = jnp.sum(pw, axis=1, keepdims=True)
            nm = jnp.dot(pw.astype(jnp.bfloat16), akv[1], preferred_element_type=jnp.float32)
            cout[:, h * DH:(h + 1) * DH] = (nm / tl).astype(jnp.bfloat16)

    context_heads(0, 4)

    load_w.wait()
    pl.semaphore_wait(zs.at[2], 2)
    drain(halves(15), g_r)
    zsrc[...] = jnp.dot(abuf[...], w[...], preferred_element_type=jnp.float32).astype(jnp.bfloat16)
    for z2, target in heads_z:
        send(zsrc.at[pl.ds(pl.multiple_of(16 * z2, 16), 16), :], zbuf.at[z], z_s, z_r, target)
    zbuf[z] = zsrc[pl.ds(pl.multiple_of(16 * z, 16), 16), :]

    context_heads(4, 8)
    store_c = local(cout, cout_hbm, osem)

    @when(sender)
    def _():
        drain(halves(15), q1_s)
        drain(kvall.at[0, pl.ds(0, 7 * 32), :], r1_s)

    @when(in_pg)
    def _():
        drain(kvall.at[0, pl.ds(0, 7 * 32), :], r2_s)
        drain(halves(7), q2_s)

    drain(kvall.at[:, pl.ds(0, 3 * BLK), :], kv_s)
    drain(half_blocks, km_s)
    drain(pbuf.at[pl.ds(0, NY - 1)], p_s)
    drain(lbuf.at[pl.ds(0, NY - 1)], l_s)
    drain(halves(15), g_s)

    @pl.when(ctx == 0)
    def _():
        drain(kvall.at[:, pl.ds(0, 7 * BLK), :], a1_s)

    @pl.when(is_source)
    def _():
        drain(kvall.at[:, pl.ds(0, 3 * BLK), :], a2_s)

    @pl.when(c == 0)
    def _():
        drain(anchor_rows, am_s)

    drain(zbuf.at[pl.ds(0, NZ - 1)], z_r)
    total = zbuf[0].astype(jnp.float32)
    for i in range(1, NZ):
        total = total + zbuf[i].astype(jnp.float32)
    qout_ref[...] = total.astype(jnp.bfloat16)
    drain(zbuf.at[pl.ds(0, NZ - 1)], z_s)
    store_c.wait()


def call(collective_id, hx, hpg, ctx_q, ctx_kv, quest_q, quest_kv, quest_len, host_block, out_weight):
    bf = jnp.bfloat16
    any_spec = pl.BlockSpec(memory_space=pl.ANY)
    smem = pl.BlockSpec(memory_space=pltpu.SMEM)
    dma = pltpu.SemaphoreType.DMA
    large = [pltpu.with_memory_space_constraint(v, pltpu.HBM) for v in (ctx_q, ctx_kv, quest_q, quest_kv, out_weight)]
    return pl.pallas_call(
        functools.partial(kernel, hx, hpg),
        out_shape=(
            jax.ShapeDtypeStruct((BLK, HEADS * DH), bf),
            jax.ShapeDtypeStruct((BLK // NZ, DH), bf),
        ),
        in_specs=[smem, smem] + [any_spec] * 5,
        out_specs=(any_spec, pl.BlockSpec(memory_space=pltpu.VMEM)),
        scratch_shapes=[
            pltpu.VMEM((BLK, HEADS * DH), bf),
            pltpu.VMEM((HEADS * DH, DH), bf),
            pltpu.VMEM((2, 2 * BLK, DH), bf),
            pltpu.VMEM((2, (ROW + 1) * BLK, DH), bf),
            pltpu.VMEM((16 if hx is None else 4, HALF, DH), bf),
            pltpu.VMEM((HALF, DH), bf),
            pltpu.VMEM((NPG if hpg is None else 1, BLK, DH), bf),
            pltpu.VMEM((8 if hx is None else 2, 32, DH), bf),
            pltpu.VMEM((32, DH), bf),
            pltpu.VMEM((BLK, DH), bf),
            pltpu.VMEM((8, BLK), jnp.float32),
            pltpu.VMEM((NY, HALF, DH), bf),
            pltpu.VMEM((NY, 8, BLK), jnp.float32),
            pltpu.VMEM((BLK, HEADS * DH), bf),
            pltpu.VMEM((BLK, DH), bf),
            pltpu.VMEM((NZ, 16, DH), bf),
            pltpu.VMEM((BLK, HEADS * DH), bf),
            dma((3,)),
            pltpu.SemaphoreType.REGULAR((3,)),
        ] + [dma] * 27,
        compiler_params=pltpu.CompilerParams(
            collective_id=collective_id, has_side_effects=True, vmem_limit_bytes=48 * 1024 * 1024
        ),
        name="star_attention",
    )(quest_len, host_block, *large)


def per_device(*args):
    return call(0, None, None, *args)


def solution(mesh):
    return jax.shard_map(
        per_device,
        mesh=mesh,
        in_specs=(
            P("ctx", "kvh"),
            P(None, "ctx", "kvh"),
            P("ctx", None, "kvh"),
            P("ctx", None, None, "kvh"),
            P(),
            P(),
            P("kvh", "ctx"),
        ),
        out_specs=(P("ctx", "kvh"), P("kvh", "ctx")),
        check_vma=False,
    )
```

```python
import functools
import math

import jax
import jax.numpy as jnp
from jax import lax
from jax.experimental import pallas as pl
from jax.experimental.pallas import tpu as pltpu
from jax.sharding import PartitionSpec as P


DH = 128
BLK = 128
HEADS = 8
HALF = 64
NX, NY, NZ = 4, 8, 8
ROW = 8
NPG = 4
MASKED = -1e30
SCALE = DH ** (-0.5)
LOG2E = math.log2(math.e)
COEF = SCALE * LOG2E
MESH = pl.DeviceIdType.MESH


def dot_t(a, b):
    return lax.dot_general(a, b, (((1,), (1,)), ((), ())), preferred_element_type=jnp.float32)


def when(cond):
    if cond is None:
        return lambda f: f()
    return pl.when(cond)


def kernel(
    hx, hpg,
    len_ref, host_ref, cq_hbm, ckv_hbm, qq_hbm, qkv_hbm, w_hbm,
    cout_hbm, qout_ref,
    cq, w, akv, kvall, q1buf, q1sel, q2buf, r1buf, r1sel, po, lsend, pbuf, lbuf, abuf, zsrc, zbuf, cout,
    lsem, zs, ys, osem, q1_s, q1_r, q2_s, q2_r, r1_s, r1_r, r2_s, r2_r, kv_s, kv_r, km_s, km_r,
    a1_s, a1_r, a2_s, a2_r, am_s, am_r, p_s, p_r, l_s, l_r, g_s, g_r, z_s, z_r,
):
    ctx = lax.axis_index("ctx")
    z = lax.axis_index("kvh")
    x = ctx // 16
    y = (ctx // 2) % NY
    c = ctx % 2
    yp = y % 2
    pg = y // 2
    head = x * 2 + c

    def at(x2, y2, c2, z2):
        return ((x2 * NY + y2) * 2 + c2, z2)

    group = []
    for dx in (2, 1, 3, 0):
        for dp in (1, 0):
            for dc in range(2):
                if dx or dp or dc:
                    x2 = (x + dx) % NX
                    yp2 = (yp + dp) % 2
                    c2 = (c + dc) % 2
                    group.append((dp, dc, x2, yp2, c2, at(x2, pg * 2 + yp2, c2, z)))
    row_members = [m[1:] for m in group if m[0] == 0]
    same_core = [m[-1] for m in row_members if m[0] == 0]
    column = [((yp + k) % 2, at(x, (y + k) % NY, c, z)) for k in (4, 3, 5, 2, 6, 1, 7)]
    heads_z = [((z + k) % NZ, at(x, y, c, (z + k) % NZ)) for k in (4, 3, 5, 2, 6, 1, 7)]
    z_near = [t for _, t in heads_z[-2:]]
    y_near = [at(x, (y + 1) % NY, c, z), at(x, (y + NY - 1) % NY, c, z)]
    y_out = at(x, (y + 2 * yp + NY - 1) % NY, c, z)
    mate = at(x, y, 1 - c, z)

    in_pg = None if hpg is None else pg == hpg
    sender = in_pg
    if hx is not None:
        sender = x == hx if sender is None else sender & (x == hx)
    q1_slots = 16 if hx is None else 4
    r1_slots = 8 if hx is None else 2
    q1_slot = c * 8 + x * 2 + yp if hx is None else c * 2 + yp
    r1_slot = c * 4 + x if hx is None else c

    def local(src, dst, sem):
        cp = pltpu.make_async_copy(src, dst, sem)
        cp.start()
        return cp

    def send(src, dst, ssem, rsem, target):
        pltpu.make_async_remote_copy(
            src_ref=src, dst_ref=dst, send_sem=ssem, recv_sem=rsem, device_id=target, device_id_type=MESH
        ).start()

    def drain(ref, sem):
        pltpu.make_async_copy(ref, ref, sem).wait()

    def halves(n):
        return kvall.at[0, pl.ds(0, n * HALF), :]

    def near_signal(sem, i, near):
        for t in near:
            pl.semaphore_signal(sem.at[i], inc=1, device_id=t, device_id_type=MESH)

    barrier = pltpu.get_barrier_semaphore()
    greet = [m[-1] for m in group] + [y_out] + z_near
    for t in greet:
        pl.semaphore_signal(barrier, inc=1, device_id=t, device_id_type=MESH)
    load_q = local(cq_hbm, cq, lsem.at[0])
    load_own = local(ckv_hbm, akv.at[:, pl.ds(BLK, BLK), :], lsem.at[1])
    load_w = local(w_hbm, w, lsem.at[2])
    pl.semaphore_wait(barrier, len(greet))
    def q_piece(x2, yp2, c2):
        return qq_hbm.at[0, pl.ds(pl.multiple_of(HALF * yp2, HALF), HALF),
                         pl.ds(pl.multiple_of(DH * (x2 * 2 + c2), DH), DH)]

    def kv_piece(x2, c2):
        first = pl.multiple_of(32 * (c2 * 2 + x2 % 2), 32)
        return qkv_hbm.at[0, x2 // 2, pl.ds(first, 32), :]

    block_rows = kvall.at[:, pl.ds(pl.multiple_of(BLK * (c * 4 + x), BLK), BLK), :]

    @when(sender)
    def _():
        for dp, dc, x2, yp2, c2, target in group:
            send(q_piece(x2, yp2, c2), q1buf.at[q1_slot], q1_s, q1_r, target)
        local(q_piece(x, yp, c), q1buf.at[q1_slot], q1_r)

    near_signal(ys, 0, y_near)

    @when(sender)
    def _():
        for dc, x2, yp2, c2, target in row_members:
            send(kv_piece(x2, c2), r1buf.at[r1_slot], r1_s, r1_r, target)
        local(kv_piece(x, c), r1buf.at[r1_slot], r1_r)

    near_signal(zs, 0, z_near)

    for target in same_core:
        send(ckv_hbm, block_rows, kv_s, kv_r, target)
    local(ckv_hbm, block_rows, kv_r)

    anchor_rows = akv.at[:, pl.ds(0, BLK), :]

    own_rows = kvall.at[:, pl.ds(ROW * BLK, BLK), :]
    r2dst = kvall.at[x // 2, pl.ds(pl.multiple_of(ROW * BLK + 32 * (c * 2 + x % 2), 32), 32), :]
    half_blocks = kvall.at[:, pl.ds(pl.multiple_of(4 * BLK * c, BLK), 4 * BLK), :]
    q2dst = q2buf.at[pg if hpg is None else 0, pl.ds(pl.multiple_of(HALF * yp, HALF), HALF), :]

    host = host_ref[0]
    length = len_ref[0]
    host_x = host // 16
    host_y = (host // 2) % NY
    host_c = host % 2
    host_yp = host_y % 2
    host_q1 = host_c * 8 + host_x * 2 + host_yp if hx is None else host_c * 2 + host_yp
    host_r1 = host_c * 4 + host_x if hx is None else host_c
    pl.semaphore_wait(ys.at[0], 2)
    near_signal(ys, 1, y_near)

    pl.semaphore_wait(ys.at[1], 2)
    near_signal(ys, 2, y_near)

    @when(in_pg)
    def _():
        drain(q1buf, q1_r)
        q1sel[...] = q1buf[host_q1]

    pl.semaphore_wait(ys.at[2], 2)

    @when(in_pg)
    def _():
        for _, target in column:
            send(q1sel, q2dst, q2_s, q2_r, target)
        local(q1sel, q2dst, q2_r)

    @when(in_pg)
    def _():
        drain(r1buf, r1_r)
        r1sel[...] = r1buf[host_r1]
        for dc, x2, yp2, c2, target in row_members:
            send(r1sel, r2dst, r2_s, r2_r, target)
        local(r1sel, r2dst, r2_r)

    @pl.when(ctx == 0)
    def _():
        for _, target in column:
            send(ckv_hbm, anchor_rows, a1_s, a1_r, target)
        local(ckv_hbm, anchor_rows, a1_r)

    if hpg is not None:
        @pl.when(pg != hpg)
        def _():
            own_rows[...] = jnp.zeros((2, BLK, DH), jnp.bfloat16)

    drain(half_blocks, kv_r)
    send(half_blocks, half_blocks, km_s, km_r, mate)

    is_source = (x == 0) & (c == 0)

    @pl.when(is_source)
    def _():
        drain(anchor_rows, a1_r)
        for target in same_core:
            send(anchor_rows, anchor_rows, a2_s, a2_r, target)

    pl.semaphore_wait(zs.at[0], 2)
    near_signal(zs, 1, z_near)

    drain(half_blocks, km_r)

    @when(in_pg)
    def _():
        drain(own_rows, r2_r)

    drain(q2buf, q2_r)

    qsel = q2buf[host_y // 2] if hpg is None else q2buf[0]
    raw = dot_t(qsel, kvall[0])
    col = lax.broadcasted_iota(jnp.int32, (BLK, BLK), 1)
    row = lax.broadcasted_iota(jnp.int32, (BLK, BLK), 0)
    limit = jnp.where(host_y == y, length, 0)
    own = jnp.where((col <= row) & (col < limit), raw[:, ROW * BLK:], MASKED)
    raw = jnp.concatenate([raw[:, : ROW * BLK], own], axis=1)
    top = jnp.max(raw, axis=1, keepdims=True)
    wts = jnp.exp2((raw - top) * COEF)
    tot = jnp.sum(wts, axis=1, keepdims=True)
    num = jnp.dot(wts.astype(jnp.bfloat16), kvall[1], preferred_element_type=jnp.float32)
    po[...] = (num / tot).astype(jnp.bfloat16)
    lse = top * COEF + jnp.log(tot) * LOG2E
    lse_row = jnp.sum(jnp.where(col == row, lse, 0.0), axis=0, keepdims=True)
    lsend[...] = lse_row
    lbuf[y] = lse_row
    for h2, target in column:
        send(lsend, lbuf.at[y], l_s, l_r, target)
        send(po.at[pl.ds(pl.multiple_of(HALF * h2, HALF), HALF), :], pbuf.at[y], p_s, p_r, target)
    pbuf[y] = po[pl.ds(pl.multiple_of(HALF * yp, HALF), HALF), :]

    @pl.when(c == 0)
    def _():
        @pl.when(jnp.logical_not(is_source))
        def _():
            drain(anchor_rows, a2_r)

        send(anchor_rows, anchor_rows, am_s, am_r, mate)

    load_q.wait()
    load_own.wait()
    pl.semaphore_wait(zs.at[1], 2)
    near_signal(zs, 2, z_near)

    drain(lbuf.at[pl.ds(0, NY - 1)], l_r)
    drain(pbuf.at[pl.ds(0, NY - 1)], p_r)
    lses = [lbuf[i] for i in range(NY)]
    best = functools.reduce(jnp.maximum, lses)
    fac = [jnp.exp2(v - best) for v in lses]
    inv = 1.0 / functools.reduce(jnp.add, fac)
    hcol = lax.broadcasted_iota(jnp.int32, (HALF, BLK), 1)
    hrow = lax.broadcasted_iota(jnp.int32, (HALF, BLK), 0) + HALF * yp
    diag = hcol == hrow
    attn = jnp.zeros((HALF, DH), jnp.float32)
    for i in range(NY):
        fcol = jnp.sum(jnp.where(diag, fac[i] * inv, 0.0), axis=1, keepdims=True)
        attn = attn + fcol * pbuf[i].astype(jnp.float32)
    attn = jnp.where(hrow < length, attn, 0.0).astype(jnp.bfloat16)
    mine = abuf.at[pl.ds(pl.multiple_of(HALF * yp, HALF), HALF), pl.ds(pl.multiple_of(DH * head, DH), DH)]
    mine[...] = attn
    for dp, dc, x2, yp2, c2, target in group:
        send(mine, mine, g_s, g_r, target)

    @pl.when(c == 1)
    def _():
        drain(anchor_rows, am_r)

    ccol = lax.broadcasted_iota(jnp.int32, (BLK, 2 * BLK), 1)
    crow = lax.broadcasted_iota(jnp.int32, (BLK, 2 * BLK), 0)
    first_visible = jnp.where(ctx > 0, 0, BLK)
    visible = (ccol >= first_visible) & (ccol - BLK <= crow)

    def context_heads(lo, hi):
        for h in range(lo, hi):
            sc = dot_t(cq[:, h * DH:(h + 1) * DH], akv[0])
            sc = jnp.where(visible, sc, MASKED)
            mx = jnp.max(sc, axis=1, keepdims=True)
            pw = jnp.exp2((sc - mx) * COEF)
            tl = jnp.sum(pw, axis=1, keepdims=True)
            nm = jnp.dot(pw.astype(jnp.bfloat16), akv[1], preferred_element_type=jnp.float32)
            cout[:, h * DH:(h + 1) * DH] = (nm / tl).astype(jnp.bfloat16)

    context_heads(0, 4)

    load_w.wait()
    pl.semaphore_wait(zs.at[2], 2)
    drain(halves(15), g_r)
    zsrc[...] = jnp.dot(abuf[...], w[...], preferred_element_type=jnp.float32).astype(jnp.bfloat16)
    for z2, target in heads_z:
        send(zsrc.at[pl.ds(pl.multiple_of(16 * z2, 16), 16), :], zbuf.at[z], z_s, z_r, target)
    zbuf[z] = zsrc[pl.ds(pl.multiple_of(16 * z, 16), 16), :]

    context_heads(4, 8)
    store_c = local(cout, cout_hbm, osem)

    @when(sender)
    def _():
        drain(halves(15), q1_s)
        drain(kvall.at[0, pl.ds(0, 7 * 32), :], r1_s)

    @when(in_pg)
    def _():
        drain(kvall.at[0, pl.ds(0, 7 * 32), :], r2_s)
        drain(halves(7), q2_s)

    drain(kvall.at[:, pl.ds(0, 3 * BLK), :], kv_s)
    drain(half_blocks, km_s)
    drain(pbuf.at[pl.ds(0, NY - 1)], p_s)
    drain(lbuf.at[pl.ds(0, NY - 1)], l_s)
    drain(halves(15), g_s)

    @pl.when(ctx == 0)
    def _():
        drain(kvall.at[:, pl.ds(0, 7 * BLK), :], a1_s)

    @pl.when(is_source)
    def _():
        drain(kvall.at[:, pl.ds(0, 3 * BLK), :], a2_s)

    @pl.when(c == 0)
    def _():
        drain(anchor_rows, am_s)

    drain(zbuf.at[pl.ds(0, NZ - 1)], z_r)
    total = zbuf[0].astype(jnp.float32)
    for i in range(1, NZ):
        total = total + zbuf[i].astype(jnp.float32)
    qout_ref[...] = total.astype(jnp.bfloat16)
    drain(zbuf.at[pl.ds(0, NZ - 1)], z_s)
    store_c.wait()


def call(collective_id, hx, hpg, ctx_q, ctx_kv, quest_q, quest_kv, quest_len, host_block, out_weight):
    bf = jnp.bfloat16
    any_spec = pl.BlockSpec(memory_space=pl.ANY)
    smem = pl.BlockSpec(memory_space=pltpu.SMEM)
    dma = pltpu.SemaphoreType.DMA
    large = [pltpu.with_memory_space_constraint(v, pltpu.HBM) for v in (ctx_q, ctx_kv, quest_q, quest_kv, out_weight)]
    return pl.pallas_call(
        functools.partial(kernel, hx, hpg),
        out_shape=(
            jax.ShapeDtypeStruct((BLK, HEADS * DH), bf),
            jax.ShapeDtypeStruct((BLK // NZ, DH), bf),
        ),
        in_specs=[smem] * 2 + [any_spec] * 5,
        out_specs=(any_spec, pl.BlockSpec(memory_space=pltpu.VMEM)),
        scratch_shapes=[
            pltpu.VMEM((BLK, HEADS * DH), bf),
            pltpu.VMEM((HEADS * DH, DH), bf),
            pltpu.VMEM((2, 2 * BLK, DH), bf),
            pltpu.VMEM((2, (ROW + 1) * BLK, DH), bf),
            pltpu.VMEM((16 if hx is None else 4, HALF, DH), bf),
            pltpu.VMEM((HALF, DH), bf),
            pltpu.VMEM((NPG if hpg is None else 1, BLK, DH), bf),
            pltpu.VMEM((8 if hx is None else 2, 32, DH), bf),
            pltpu.VMEM((32, DH), bf),
            pltpu.VMEM((BLK, DH), bf),
            pltpu.VMEM((1, BLK), jnp.float32),
            pltpu.VMEM((NY, HALF, DH), bf),
            pltpu.VMEM((NY, 1, BLK), jnp.float32),
            pltpu.VMEM((BLK, HEADS * DH), bf),
            pltpu.VMEM((BLK, DH), bf),
            pltpu.VMEM((NZ, 16, DH), bf),
            pltpu.VMEM((BLK, HEADS * DH), bf),
            dma((3,)),
            pltpu.SemaphoreType.REGULAR((3,)),
            pltpu.SemaphoreType.REGULAR((3,)),
        ] + [dma] * 27,
        compiler_params=pltpu.CompilerParams(
            collective_id=collective_id, has_side_effects=True, vmem_limit_bytes=48 * 1024 * 1024
        ),
        name="star_attention",
    )(quest_len, host_block, *large)


def per_device(*args):
    return call(0, None, None, *args)


def solution(mesh):
    return jax.shard_map(
        per_device,
        mesh=mesh,
        in_specs=(
            P("ctx", "kvh"),
            P(None, "ctx", "kvh"),
            P("ctx", None, "kvh"),
            P("ctx", None, None, "kvh"),
            P(),
            P(),
            P("kvh", "ctx"),
        ),
        out_specs=(P("ctx", "kvh"), P("kvh", "ctx")),
        check_vma=False,
    )
```

```python
import functools
import math

import jax
import jax.numpy as jnp
from jax import lax
from jax.experimental import pallas as pl
from jax.experimental.pallas import tpu as pltpu
from jax.sharding import PartitionSpec as P


DH = 128
BLK = 128
HEADS = 8
HALF = 64
NX, NY, NZ = 4, 8, 8
ROW = 8
NPG = 4
MASKED = -1e30
SCALE = DH ** (-0.5)
LOG2E = math.log2(math.e)
COEF = SCALE * LOG2E
MESH = pl.DeviceIdType.MESH


def dot_t(a, b):
    return lax.dot_general(a, b, (((1,), (1,)), ((), ())), preferred_element_type=jnp.float32)


def when(cond):
    if cond is None:
        return lambda f: f()
    return pl.when(cond)


def kernel(
    hx, hpg,
    len_ref, host_ref, cq_hbm, ckv_hbm, qq_hbm, qkv_hbm, w_hbm,
    cout_hbm, qout_ref,
    cq, w, akv, kvall, q1buf, q1sel, q2buf, r1buf, r1sel, po, lsend, pbuf, lbuf, abuf, zsrc, zbuf, cout,
    lsem, zs, ys, osem, q1_s, q1_r, q2_s, q2_r, r1_s, r1_r, r2_s, r2_r, kv_s, kv_r, km_s, km_r,
    a1_s, a1_r, a2_s, a2_r, am_s, am_r, p_s, p_r, l_s, l_r, g_s, g_r, z_s, z_r,
):
    ctx = lax.axis_index("ctx")
    z = lax.axis_index("kvh")
    x = ctx // 16
    y = (ctx // 2) % NY
    c = ctx % 2
    yp = y % 2
    pg = y // 2
    head = x * 2 + c

    def at(x2, y2, c2, z2):
        return ((x2 * NY + y2) * 2 + c2, z2)

    group = []
    for dx in (2, 1, 3, 0):
        for dp in (1, 0):
            for dc in range(2):
                if dx or dp or dc:
                    x2 = (x + dx) % NX
                    yp2 = (yp + dp) % 2
                    c2 = (c + dc) % 2
                    group.append((dp, dc, x2, yp2, c2, at(x2, pg * 2 + yp2, c2, z)))
    row_members = [m[1:] for m in group if m[0] == 0]
    same_core = [m[-1] for m in row_members if m[0] == 0]
    column = [((yp + k) % 2, at(x, (y + k) % NY, c, z)) for k in (4, 3, 5, 2, 6, 1, 7)]
    heads_z = [((z + k) % NZ, at(x, y, c, (z + k) % NZ)) for k in (4, 3, 5, 2, 6, 1, 7)]
    z_near = [t for _, t in heads_z[-2:]]
    y_near = [at(x, (y + 1) % NY, c, z), at(x, (y + NY - 1) % NY, c, z)]
    y_out = at(x, (y + 2 * yp + NY - 1) % NY, c, z)
    mate = at(x, y, 1 - c, z)

    in_pg = None if hpg is None else pg == hpg
    sender = in_pg
    if hx is not None:
        sender = x == hx if sender is None else sender & (x == hx)
    q1_slots = 16 if hx is None else 4
    r1_slots = 8 if hx is None else 2
    q1_slot = c * 8 + x * 2 + yp if hx is None else c * 2 + yp
    r1_slot = c * 4 + x if hx is None else c

    def local(src, dst, sem):
        cp = pltpu.make_async_copy(src, dst, sem)
        cp.start()
        return cp

    def send(src, dst, ssem, rsem, target):
        pltpu.make_async_remote_copy(
            src_ref=src, dst_ref=dst, send_sem=ssem, recv_sem=rsem, device_id=target, device_id_type=MESH
        ).start()

    def drain(ref, sem):
        pltpu.make_async_copy(ref, ref, sem).wait()

    def halves(n):
        return kvall.at[0, pl.ds(0, n * HALF), :]

    def near_signal(sem, i, near):
        for t in near:
            pl.semaphore_signal(sem.at[i], inc=1, device_id=t, device_id_type=MESH)

    barrier = pltpu.get_barrier_semaphore()
    greet = [m[-1] for m in group] + [y_out] + z_near
    for t in greet:
        pl.semaphore_signal(barrier, inc=1, device_id=t, device_id_type=MESH)
    load_q = local(cq_hbm, cq, lsem.at[0])
    load_own = local(ckv_hbm, akv.at[:, pl.ds(BLK, BLK), :], lsem.at[1])
    load_w = local(w_hbm, w, lsem.at[2])
    pl.semaphore_wait(barrier, len(greet))
    def q_piece(x2, yp2, c2):
        return qq_hbm.at[0, pl.ds(pl.multiple_of(HALF * yp2, HALF), HALF),
                         pl.ds(pl.multiple_of(DH * (x2 * 2 + c2), DH), DH)]

    def kv_piece(x2, c2):
        first = pl.multiple_of(32 * (c2 * 2 + x2 % 2), 32)
        return qkv_hbm.at[0, x2 // 2, pl.ds(first, 32), :]

    block_rows = kvall.at[:, pl.ds(pl.multiple_of(BLK * (c * 4 + x), BLK), BLK), :]

    @when(sender)
    def _():
        for dp, dc, x2, yp2, c2, target in group:
            send(q_piece(x2, yp2, c2), q1buf.at[q1_slot], q1_s, q1_r, target)
        local(q_piece(x, yp, c), q1buf.at[q1_slot], q1_r)

    near_signal(ys, 0, y_near)

    @when(sender)
    def _():
        for dc, x2, yp2, c2, target in row_members:
            send(kv_piece(x2, c2), r1buf.at[r1_slot], r1_s, r1_r, target)
        local(kv_piece(x, c), r1buf.at[r1_slot], r1_r)

    near_signal(zs, 0, z_near)

    for target in same_core:
        send(ckv_hbm, block_rows, kv_s, kv_r, target)
    local(ckv_hbm, block_rows, kv_r)

    anchor_rows = akv.at[:, pl.ds(0, BLK), :]

    own_rows = kvall.at[:, pl.ds(ROW * BLK, BLK), :]
    r2dst = kvall.at[x // 2, pl.ds(pl.multiple_of(ROW * BLK + 32 * (c * 2 + x % 2), 32), 32), :]
    half_blocks = kvall.at[:, pl.ds(pl.multiple_of(4 * BLK * c, BLK), 4 * BLK), :]
    q2dst = q2buf.at[pg if hpg is None else 0, pl.ds(pl.multiple_of(HALF * yp, HALF), HALF), :]

    host = host_ref[0]
    length = len_ref[0]
    host_x = host // 16
    host_y = (host // 2) % NY
    host_c = host % 2
    host_yp = host_y % 2
    host_q1 = host_c * 8 + host_x * 2 + host_yp if hx is None else host_c * 2 + host_yp
    host_r1 = host_c * 4 + host_x if hx is None else host_c
    pl.semaphore_wait(ys.at[0], 2)
    near_signal(ys, 1, y_near)

    pl.semaphore_wait(ys.at[1], 2)
    near_signal(ys, 2, y_near)

    @when(in_pg)
    def _():
        drain(q1buf, q1_r)
        q1sel[...] = q1buf[host_q1]

    pl.semaphore_wait(ys.at[2], 2)

    @when(in_pg)
    def _():
        for _, target in column:
            send(q1sel, q2dst, q2_s, q2_r, target)
        local(q1sel, q2dst, q2_r)

    @when(in_pg)
    def _():
        drain(r1buf, r1_r)
        r1sel[...] = r1buf[host_r1]
        for dc, x2, yp2, c2, target in row_members:
            send(r1sel, r2dst, r2_s, r2_r, target)
        local(r1sel, r2dst, r2_r)

    @pl.when(ctx == 0)
    def _():
        for _, target in column:
            send(ckv_hbm, anchor_rows, a1_s, a1_r, target)
        local(ckv_hbm, anchor_rows, a1_r)

    if hpg is not None:
        @pl.when(pg != hpg)
        def _():
            own_rows[...] = jnp.zeros((2, BLK, DH), jnp.bfloat16)

    drain(half_blocks, kv_r)
    send(half_blocks, half_blocks, km_s, km_r, mate)

    is_source = (x == 0) & (c == 0)

    pl.semaphore_wait(zs.at[0], 2)
    near_signal(zs, 1, z_near)

    drain(half_blocks, km_r)

    @when(in_pg)
    def _():
        drain(own_rows, r2_r)

    drain(q2buf, q2_r)

    qsel = q2buf[host_y // 2] if hpg is None else q2buf[0]
    raw = dot_t(qsel, kvall[0])
    col = lax.broadcasted_iota(jnp.int32, (BLK, BLK), 1)
    row = lax.broadcasted_iota(jnp.int32, (BLK, BLK), 0)
    limit = jnp.where(host_y == y, length, 0)
    own = jnp.where((col <= row) & (col < limit), raw[:, ROW * BLK:], MASKED)
    raw = jnp.concatenate([raw[:, : ROW * BLK], own], axis=1)
    top = jnp.max(raw, axis=1, keepdims=True)
    wts = jnp.exp2((raw - top) * COEF)
    tot = jnp.sum(wts, axis=1, keepdims=True)
    num = jnp.dot(wts.astype(jnp.bfloat16), kvall[1], preferred_element_type=jnp.float32)
    po[...] = (num / tot).astype(jnp.bfloat16)
    lse = top * COEF + jnp.log(tot) * LOG2E
    lse_row = jnp.sum(jnp.where(col == row, lse, 0.0), axis=0, keepdims=True)
    lsend[...] = lse_row
    lbuf[y] = lse_row
    for y2 in (0, 1, 7, 2, 6, 3, 5, 4):
        @pl.when(y2 != y)
        def _(y2=y2):
            send(lsend, lbuf.at[y], l_s, l_r, at(x, y2, c, z))
            send(po.at[pl.ds(HALF * (y2 % 2), HALF), :], pbuf.at[y], p_s, p_r, at(x, y2, c, z))

    pbuf[y] = po[pl.ds(pl.multiple_of(HALF * yp, HALF), HALF), :]

    @pl.when(is_source)
    def _():
        drain(anchor_rows, a1_r)
        for target in same_core:
            send(anchor_rows, anchor_rows, a2_s, a2_r, target)

    load_q.wait()
    load_own.wait()
    pl.semaphore_wait(zs.at[1], 2)
    near_signal(zs, 2, z_near)

    drain(lbuf.at[pl.ds(0, NY - 1)], l_r)
    drain(pbuf.at[pl.ds(0, NY - 1)], p_r)
    lses = [lbuf[i] for i in range(NY)]
    best = functools.reduce(jnp.maximum, lses)
    fac = [jnp.exp2(v - best) for v in lses]
    inv = 1.0 / functools.reduce(jnp.add, fac)
    hcol = lax.broadcasted_iota(jnp.int32, (HALF, BLK), 1)
    hrow = lax.broadcasted_iota(jnp.int32, (HALF, BLK), 0) + HALF * yp
    diag = hcol == hrow
    attn = jnp.zeros((HALF, DH), jnp.float32)
    for i in range(NY):
        fcol = jnp.sum(jnp.where(diag, fac[i] * inv, 0.0), axis=1, keepdims=True)
        attn = attn + fcol * pbuf[i].astype(jnp.float32)
    attn = jnp.where(hrow < length, attn, 0.0).astype(jnp.bfloat16)
    mine = abuf.at[pl.ds(pl.multiple_of(HALF * yp, HALF), HALF), pl.ds(pl.multiple_of(DH * head, DH), DH)]
    mine[...] = attn
    for x2, yp2, c2 in [(x2, yp2, c2) for x2 in (0, 1, 3, 2) for yp2 in range(2) for c2 in (1, 0)]:
        @pl.when((x2 != x) | (yp2 != yp) | (c2 != c))
        def _(x2=x2, yp2=yp2, c2=c2):
            send(mine, mine, g_s, g_r, at(x2, pg * 2 + yp2, c2, z))


    @pl.when(c == 0)
    def _():
        @pl.when(jnp.logical_not(is_source))
        def _():
            drain(anchor_rows, a2_r)

        send(anchor_rows, anchor_rows, am_s, am_r, mate)

    ccol = lax.broadcasted_iota(jnp.int32, (BLK, 2 * BLK), 1)
    crow = lax.broadcasted_iota(jnp.int32, (BLK, 2 * BLK), 0)
    first_visible = jnp.where(ctx > 0, 0, BLK)
    visible = (ccol >= first_visible) & (ccol - BLK <= crow)

    def context_heads(lo, hi):
        for h in range(lo, hi):
            sc = dot_t(cq[:, h * DH:(h + 1) * DH], akv[0])
            sc = jnp.where(visible, sc, MASKED)
            mx = jnp.max(sc, axis=1, keepdims=True)
            pw = jnp.exp2((sc - mx) * COEF)
            tl = jnp.sum(pw, axis=1, keepdims=True)
            nm = jnp.dot(pw.astype(jnp.bfloat16), akv[1], preferred_element_type=jnp.float32)
            cout[:, h * DH:(h + 1) * DH] = (nm / tl).astype(jnp.bfloat16)

    load_w.wait()
    pl.semaphore_wait(zs.at[2], 2)
    drain(halves(15), g_r)
    zsrc[...] = jnp.dot(abuf[...], w[...], preferred_element_type=jnp.float32).astype(jnp.bfloat16)
    for z2 in range(NZ):
        @pl.when(z2 != z)
        def _(z2=z2):
            send(zsrc.at[pl.ds(16 * z2, 16), :], zbuf.at[z], z_s, z_r, at(x, y, c, z2))

    zbuf[z] = zsrc[pl.ds(pl.multiple_of(16 * z, 16), 16), :]

    @pl.when(c == 1)
    def _():
        drain(anchor_rows, am_r)

    context_heads(0, 8)
    store_c = local(cout, cout_hbm, osem)

    @when(sender)
    def _():
        drain(halves(15), q1_s)
        drain(kvall.at[0, pl.ds(0, 7 * 32), :], r1_s)

    @when(in_pg)
    def _():
        drain(kvall.at[0, pl.ds(0, 7 * 32), :], r2_s)
        drain(halves(7), q2_s)

    drain(kvall.at[:, pl.ds(0, 3 * BLK), :], kv_s)
    drain(half_blocks, km_s)
    drain(pbuf.at[pl.ds(0, NY - 1)], p_s)
    drain(lbuf.at[pl.ds(0, NY - 1)], l_s)
    drain(halves(15), g_s)

    @pl.when(ctx == 0)
    def _():
        drain(kvall.at[:, pl.ds(0, 7 * BLK), :], a1_s)

    @pl.when(is_source)
    def _():
        drain(kvall.at[:, pl.ds(0, 3 * BLK), :], a2_s)

    @pl.when(c == 0)
    def _():
        drain(anchor_rows, am_s)

    drain(zbuf.at[pl.ds(0, NZ - 1)], z_r)
    total = zbuf[0].astype(jnp.float32)
    for i in range(1, NZ):
        total = total + zbuf[i].astype(jnp.float32)
    qout_ref[...] = total.astype(jnp.bfloat16)
    drain(zbuf.at[pl.ds(0, NZ - 1)], z_s)
    store_c.wait()


def call(collective_id, hx, hpg, ctx_q, ctx_kv, quest_q, quest_kv, quest_len, host_block, out_weight):
    bf = jnp.bfloat16
    any_spec = pl.BlockSpec(memory_space=pl.ANY)
    smem = pl.BlockSpec(memory_space=pltpu.SMEM)
    dma = pltpu.SemaphoreType.DMA
    large = [pltpu.with_memory_space_constraint(v, pltpu.HBM) for v in (ctx_q, ctx_kv, quest_q, quest_kv, out_weight)]
    return pl.pallas_call(
        functools.partial(kernel, hx, hpg),
        out_shape=(
            jax.ShapeDtypeStruct((BLK, HEADS * DH), bf),
            jax.ShapeDtypeStruct((BLK // NZ, DH), bf),
        ),
        in_specs=[smem] * 2 + [any_spec] * 5,
        out_specs=(any_spec, pl.BlockSpec(memory_space=pltpu.VMEM)),
        scratch_shapes=[
            pltpu.VMEM((BLK, HEADS * DH), bf),
            pltpu.VMEM((HEADS * DH, DH), bf),
            pltpu.VMEM((2, 2 * BLK, DH), bf),
            pltpu.VMEM((2, (ROW + 1) * BLK, DH), bf),
            pltpu.VMEM((16 if hx is None else 4, HALF, DH), bf),
            pltpu.VMEM((HALF, DH), bf),
            pltpu.VMEM((NPG if hpg is None else 1, BLK, DH), bf),
            pltpu.VMEM((8 if hx is None else 2, 32, DH), bf),
            pltpu.VMEM((32, DH), bf),
            pltpu.VMEM((BLK, DH), bf),
            pltpu.VMEM((1, BLK), jnp.float32),
            pltpu.VMEM((NY, HALF, DH), bf),
            pltpu.VMEM((NY, 1, BLK), jnp.float32),
            pltpu.VMEM((BLK, HEADS * DH), bf),
            pltpu.VMEM((BLK, DH), bf),
            pltpu.VMEM((NZ, 16, DH), bf),
            pltpu.VMEM((BLK, HEADS * DH), bf),
            dma((3,)),
            pltpu.SemaphoreType.REGULAR((3,)),
            pltpu.SemaphoreType.REGULAR((3,)),
        ] + [dma] * 27,
        compiler_params=pltpu.CompilerParams(
            collective_id=collective_id, has_side_effects=True, vmem_limit_bytes=48 * 1024 * 1024
        ),
        name="star_attention",
    )(quest_len, host_block, *large)


def per_device(*args):
    return call(0, None, None, *args)


def solution(mesh):
    return jax.shard_map(
        per_device,
        mesh=mesh,
        in_specs=(
            P("ctx", "kvh"),
            P(None, "ctx", "kvh"),
            P("ctx", None, "kvh"),
            P("ctx", None, None, "kvh"),
            P(),
            P(),
            P("kvh", "ctx"),
        ),
        out_specs=(P("ctx", "kvh"), P("kvh", "ctx")),
        check_vma=False,
    )
```
